32 devices in a mesh: tm: 4 (over y, x), gx: 4 (over z), gy: 2 (over core).
Axes of the slice: x: 2, y: 2, z: 4, core: 2. Of those that a mesh axis runs over, the one named last changes fastest.
Arguments:
- slice_starts: float32 [4, 64, 32, 256], P('tm', 'gx', 'gy'), may hold values from -2.5 to 4, as said below
- material: int32 [64, 32, 256], P('gx', 'gy'), may hold values from 0 to 7
- conduct_table: float32 [8], replicated, may hold values from 0.5 to 1
- wall_flags: int32 [2, 64, 32], P(None, 'gx', 'gy'), may hold values 0 or 1
- pod_basis: bfloat16 [128, 64, 32, 256], P('tm', 'gx', 'gy'), may hold values from -0.0078125 to 0.0078125
Outputs:
- slice_ends: float32 [4, 64, 32, 256], P('tm', 'gx', 'gy')
- pod_coeffs: float32 [4, 128], P(None, 'tm')
The draws below stay inside these ranges and needn't reach their ends.
Inputs may be any that keep to these rules, and one draw needn't show every extreme that they name: `slice_starts`: start temperatures.
All inputs are finite; a program needn't handle non-finite values. No bound on the sum of `wall_flags` on one device may be relied on, other than what follows from the above.
Results may differ from the reference program's by a relative error of at most 0.0003.
Values may be sent and summed in bfloat16 or wider, within the bound.
A program may use at most 64 MiB of HBM per device.

```python
import math
import jax
import jax.numpy as jnp
from jax import lax

NZ = 256
STEPS = 8
CSTEPS = 1
MODES = 128
REGIONS = 8
NX = 64
NY = 32
SLICES = 4


def draw_slice_starts(key, part):
    shape = (SLICES, NX, NY, NZ)
    values = jnp.clip(1.0 + 1.5 * jax.random.normal(key, shape, jnp.float32), -2.5, 4.0)
    return values.astype(jnp.float32)


def plant(result, own_key, smallest, high):
    longest = result.shape.index(max(result.shape))
    spots = []
    for shift in (0, 1):
        where = [jax.random.randint(jax.random.fold_in(own_key, axis), (), 0, length) for axis, length in enumerate(result.shape)]
        where[longest] = (where[longest] + shift) % result.shape[longest]
        spots.append(tuple(where))
    return result.at[spots[0]].set(smallest).at[spots[1]].set(high)


def shard_levels(rng, shape, pieces, least, top_value):
    loudness = 1.0
    for dim, shards_of in pieces:
        steps = jax.random.uniform(jax.random.fold_in(jax.random.fold_in(rng, 6), dim), (shards_of,), jnp.float32, least / len(pieces), top_value / len(pieces))
        loudness = loudness * jnp.repeat(jnp.exp(steps), shape[dim] // shards_of).reshape((-1,) + (1,) * (len(shape) - 1 - dim))
    return loudness


def gaussian(stream_key, shape, scale, bound, shards=(), kind=jnp.bfloat16):
    array = jax.random.normal(stream_key, shape, jnp.float32) * scale
    if len(shards) > 0:
        array = shard_levels(stream_key, shape, shards, -0.22, 0.18) * array
    return jnp.clip(array, min=-bound, max=bound).astype(kind)


def setup_inputs(seed: int = 0) -> dict:
    splits = jax.random.split(jax.random.key(seed), 6)
    slice_starts = draw_slice_starts(jax.random.fold_in(splits[5], 71), 0)
    material = plant(jax.random.randint(splits[1], (NX, NY, NZ), 0, REGIONS), jax.random.fold_in(splits[1], 1), 0, REGIONS - 1).astype(jnp.int32)
    conduct_table = jnp.clip(jnp.exp(jax.random.uniform(splits[2], (REGIONS,), jnp.float32, math.log(0.5), math.log(1.0))), 0.5, 1.0)
    wall_flags = plant((jax.random.randint(splits[3], (2, NX, NY), 0, 2) < 1).astype(jnp.int32), jax.random.fold_in(splits[3], 1), 0, 1)
    pod_basis = gaussian(splits[4], (MODES, NX, NY, NZ), (NX * NY * NZ) ** -0.5, 0.0078125, ((0, 4), (1, 4), (2, 2)))
    return {"slice_starts": slice_starts, "material": material, "conduct_table": conduct_table, "wall_flags": wall_flags, "pod_basis": pod_basis}


fine_rate = 0.1
coarse_rate = 0.05


def face(k_here, k_there):
    return 2.0 * k_here * k_there / jnp.maximum(k_here + k_there, 1.0)


def step_region(upad, kstat, rate):
    kval = kstat * (1.0 + 0.5 * jnp.tanh(upad))
    center = upad[1:-1, 1:-1, 1:-1]
    kcen = kval[1:-1, 1:-1, 1:-1]
    beside_all = [
        (slice(2, None), slice(1, -1), slice(1, -1)),
        (slice(0, -2), slice(1, -1), slice(1, -1)),
        (slice(1, -1), slice(2, None), slice(1, -1)),
        (slice(1, -1), slice(0, -2), slice(1, -1)),
        (slice(1, -1), slice(1, -1), slice(2, None)),
        (slice(1, -1), slice(1, -1), slice(0, -2)),
    ]
    total = jnp.zeros_like(center)
    for where_at in beside_all:
        total = total + face(kcen, kval[where_at]) * (upad[where_at] - center)
    return center + rate * total


def lookup(material, conduct_table):
    coef = jnp.zeros(material.shape, jnp.float32)
    for region in range(conduct_table.shape[0]):
        coef = coef + jnp.where(material == region, conduct_table[region], 0.0)
    return coef


def restrict(field):
    a, b, c = field.shape
    return jnp.mean(field.reshape(a // 4, 4, b // 4, 4, c // 4, 4), axis=(1, 3, 5))


def prolong(field):
    return jnp.repeat(jnp.repeat(jnp.repeat(field, 4, axis=0), 4, axis=1), 4, axis=2)


def pad_all(field):
    return jnp.pad(field, ((1, 1), (1, 1), (1, 1)))


def pad_side(field):
    return jnp.pad(field, ((1, 1), (1, 1), (0, 0)))


def reference(slice_starts, material, conduct_table, wall_flags, pod_basis):
    coef = lookup(material, conduct_table)
    lower = wall_flags[0].astype(jnp.float32)
    upper = wall_flags[1].astype(jnp.float32)
    packed = jnp.concatenate([(lower * coef[:, :, 0])[:, :, None], coef, (upper * coef[:, :, -1])[:, :, None]], axis=2)
    packed_ext = pad_side(packed)
    coarse_ext = pad_all(restrict(coef))

    def fine(state):
        for step in range(STEPS):
            state = step_region(pad_all(state), packed_ext, fine_rate)
        return state

    def coarse(field):
        for step in range(CSTEPS):
            field = step_region(pad_all(field), coarse_ext, coarse_rate)
        return field

    def propagate(state):
        return prolong(coarse(restrict(state)))

    slices = slice_starts.shape[0]
    jumps = [fine(slice_starts[n]) - propagate(slice_starts[n]) for n in range(slices)]
    current = slice_starts[0]
    ends = []
    coeffs = []
    flat_basis = pod_basis.reshape(pod_basis.shape[0], -1)
    for n in range(slices):
        current = propagate(current) + jumps[n]
        ends.append(current)
        ends_high = lax.optimization_barrier(current.astype(jnp.bfloat16))
        left_over = current - ends_high.astype(jnp.float32)
        ends_rest = lax.optimization_barrier(left_over.astype(jnp.bfloat16))
        ends_low = (left_over - ends_rest.astype(jnp.float32)).astype(jnp.bfloat16)
        first = jnp.dot(flat_basis, ends_high.reshape(-1), preferred_element_type=jnp.float32)
        second = jnp.dot(flat_basis, ends_rest.reshape(-1), preferred_element_type=jnp.float32)
        third = jnp.dot(flat_basis, ends_low.reshape(-1), preferred_element_type=jnp.float32)
        coeffs.append(first + second + third)
    return jnp.stack(ends), jnp.stack(coeffs)
```

```python
import functools

import jax
import jax.numpy as jnp
from jax import lax
from jax.experimental import pallas as pl
from jax.experimental.pallas import tpu as pltpu
from jax.sharding import PartitionSpec as P

STEPS = 8
W = 4
YP = 8

fine_rate = 0.1
coarse_rate = 0.05

MESH = pl.DeviceIdType.MESH
F32 = jnp.float32
HIGH = lax.Precision.HIGHEST
AROUND = [(a, b) for a in (-1, 0, 1) for b in (-1, 0, 1) if (a, b) != (0, 0)]


def conduct(k_here, k_there):
    bottom = jnp.maximum(k_here + k_there, 1.0)
    return k_here * k_there * pl.reciprocal(bottom, approx=True)


def conduct_exact(k_here, k_there):
    return k_here * k_there / jnp.maximum(k_here + k_there, 1.0)


def iota(shape, dim):
    return lax.broadcasted_iota(jnp.int32, shape, dim)


def mm(a, b):
    return lax.dot_general(a, b, (((1,), (0,)), ((), ())), precision=HIGH, preferred_element_type=F32)


def kernel(sizes, start, material, table, walls, out, means,
           A, B, C, S, SA, KG, K, h_send, h_recv):
    nt, ngx, ngy = sizes
    bx, by, nz = material.shape
    ex, ey = bx + 2 * W, by + 2 * YP
    cx, cy = bx // 4, by // 4
    crows = cx * cy
    t, gx, gy = lax.axis_index("tm"), lax.axis_index("gx"), lax.axis_index("gy")

    def exists(a, b):
        ok = None
        for d, g, n in ((a, gx, ngx), (b, gy, ngy)):
            if d:
                this = (g + d >= 0) & (g + d < n)
                ok = this if ok is None else ok & this
        return ok

    def if_there(a, b, extra=None):
        ok = exists(a, b)
        if extra is not None:
            ok = extra if ok is None else ok & extra
        return pl.when(ok) if ok is not None else (lambda f: f())

    barrier = pltpu.get_barrier_semaphore()
    for a, b in AROUND:
        @if_there(a, b)
        def _():
            pl.semaphore_signal(barrier, inc=1, device_id={"tm": t, "gx": gx + a, "gy": gy + b}, device_id_type=MESH)

    for a, xs in ((-1, slice(0, W)), (1, slice(W + bx, ex))):
        @pl.when(jnp.logical_not(exists(a, 0)))
        def _():
            for ref in (A, C, S):
                ref[xs] = jnp.zeros((W, ey, nz), F32)
    for b, ys in ((-1, slice(0, YP)), (1, slice(YP + by, ey))):
        @pl.when(jnp.logical_not(exists(0, b)))
        def _():
            for ref in (A, C, S):
                ref[:, ys, :] = jnp.zeros((ex, YP, nz), F32)
    lane = iota((by, nz), 1)
    eye = iota((by, by), 0) == iota((by, by), 1)

    @pl.loop(0, bx)
    def _(x):
        mat = material[x]
        coef = jnp.zeros((by, nz), F32)
        for region in range(table.shape[0]):
            coef = jnp.where(mat == region, table[region], coef)
        low = jnp.sum(jnp.where(eye, walls[0, pl.ds(x, 1), :].astype(F32), 0.0), axis=1, keepdims=True)
        top = jnp.sum(jnp.where(eye, walls[1, pl.ds(x, 1), :].astype(F32), 0.0), axis=1, keepdims=True)
        flag = jnp.where(lane == 0, low, jnp.where(lane == nz - 1, top, 0.0))
        S[W + x, YP:YP + by, :] = jnp.where(flag > 0.5, -coef, coef)
        A[W + x, YP:YP + by, :] = start[0, x]

    rows_p = (cx * cy, cx * by)
    gather_rows = jnp.where(
        (iota(rows_p, 0) // cy == iota(rows_p, 1) // by) & (iota(rows_p, 0) % cy == (iota(rows_p, 1) % by) // 4), 1.0, 0.0)
    gather_lanes = jnp.where(iota((nz, 128), 0) // 4 == iota((nz, 128), 1), 1.0 / 64.0, 0.0)
    def restrict(cell):
        slabs = []
        for X in range(cx):
            slabs.append((cell(4 * X) + cell(4 * X + 1)) + (cell(4 * X + 2) + cell(4 * X + 3)))
        return mm(mm(gather_rows, jnp.concatenate(slabs, axis=0)), gather_lanes)

    pl.semaphore_wait(barrier, (1 + (gx > 0).astype(jnp.int32) + (gx < ngx - 1).astype(jnp.int32))
                      * (1 + (gy > 0).astype(jnp.int32) + (gy < ngy - 1).astype(jnp.int32)) - 1)

    def halo(ref, kind, i, a, b):
        xs = {-1: (W, W + bx, W), 0: (W, W, bx), 1: (bx, 0, W)}[a]
        ys = {-1: (YP, YP + by, YP), 0: (YP, YP, by), 1: (by, 0, YP)}[b]
        return pltpu.make_async_remote_copy(
            src_ref=ref.at[pl.ds(xs[0], xs[2]), pl.ds(ys[0], ys[2]), :],
            dst_ref=ref.at[pl.ds(xs[1], xs[2]), pl.ds(ys[1], ys[2]), :],
            send_sem=h_send.at[kind, i],
            recv_sem=h_recv.at[kind, i],
            device_id={"tm": t, "gx": gx + a, "gy": gy + b},
            device_id_type=MESH,
        )

    def send_halo(ref, kind):
        for i, (a, b) in enumerate(AROUND):
            @if_there(a, b)
            def _():
                halo(ref, kind, i, a, b).start()

    def left_halo(ref, kind):
        for i, (a, b) in enumerate(AROUND):
            @if_there(a, b)
            def _():
                halo(ref, kind, i, a, b).wait_send()

    def land_halo(ref, kind):
        for i, (a, b) in enumerate(AROUND):
            @if_there(-a, -b)
            def _():
                xs = {-1: (W + bx, W), 0: (W, bx), 1: (0, W)}[a]
                ys = {-1: (YP + by, YP), 0: (YP, by), 1: (0, YP)}[b]
                spot = ref.at[pl.ds(xs[0], xs[1]), pl.ds(ys[0], ys[1]), :]
                pltpu.make_async_remote_copy(
                    src_ref=spot, dst_ref=spot, send_sem=h_send.at[kind, i], recv_sem=h_recv.at[kind, i],
                    device_id={"tm": t, "gx": gx - a, "gy": gy - b}, device_id_type=MESH,
                ).wait_recv()

    send_halo(A, 0)
    send_halo(S, 1)

    own = slice(YP, YP + by)
    means[0:crows, :] = restrict(lambda x: A[W + x, own, :])
    means[crows:2 * crows, :] = restrict(lambda x: jnp.abs(S[W + x, own, :]))

    def conductivity(src, r):
        @pl.loop(W - r - 1, W + bx + r + 1)
        def _(x):
            K[x] = SA[x] * (1.0 + 0.5 * jnp.tanh(src[x]))

    def step(src, put, r):
        conductivity(src, r)
        ylo, yhi = (YP, YP + by) if r == 0 else (YP - 4, YP + by + 4)
        rows = slice(ylo, yhi)
        last = iota((yhi - ylo, nz), 1) == nz - 1

        def body(x, carry):
            kc, uc, fxm = carry
            kn, un = K[x + 1, rows, :], src[x + 1, rows, :]
            fx = conduct(kc, kn) * (un - uc)
            total = fx - fxm
            total += conduct(kc, K[x, ylo + 1:yhi + 1, :]) * (src[x, ylo + 1:yhi + 1, :] - uc)
            total += conduct(kc, K[x, ylo - 1:yhi - 1, :]) * (src[x, ylo - 1:yhi - 1, :] - uc)
            fz = conduct(kc, pltpu.roll(kc, nz - 1, 1)) * (pltpu.roll(uc, nz - 1, 1) - uc)
            fz = jnp.where(last, 0.0, fz)
            total += fz - pltpu.roll(fz, 1, 1)
            total -= conduct(kc, KG[x, rows, :]) * uc
            put(x, rows, uc + (2.0 * fine_rate) * total)
            return kn, un, fx

        x0 = W - r
        k0, u0 = K[x0, rows, :], src[x0, rows, :]
        k1, u1 = K[x0 - 1, rows, :], src[x0 - 1, rows, :]
        lax.fori_loop(x0, W + bx + r, body, (k0, u0, conduct(k0, k1) * (u0 - u1)))

    def into(ref):
        def put(x, rows, value):
            ref[x, rows, :] = value
        return put

    def into_out(x, rows, value):
        out[0, x - W] = value

    land_halo(A, 0)
    land_halo(S, 1)

    @pl.loop(0, ex)
    def _(x):
        s = S[x]
        SA[x] = jnp.abs(s)
        KG[x] = jnp.where(s < 0.0, -s, 0.0)

    def exchange_then(src, kind):
        send_halo(src, kind)
        land_halo(src, kind)

    step(A, into(B), 3)
    left_halo(A, 0)
    step(B, into(A), 2)
    step(A, into(B), 1)
    step(B, into(C), 0)
    exchange_then(C, 2)
    step(C, into(B), 3)
    step(B, into(A), 2)
    step(A, into(B), 1)

    step(B, into_out, 0)
    means[2 * crows:, :] = restrict(lambda x: out[0, x])
    left_halo(S, 1)
    left_halo(C, 2)


def finish(cy, ends, change, out):
    bx, by, nz = ends.shape[1:]
    cx = bx // 4
    shape = (cx * by, cx * cy)
    spread_rows = jnp.where(
        (iota(shape, 1) // cy == iota(shape, 0) // by) & (iota(shape, 1) % cy == (iota(shape, 0) % by) // 4), 1.0, 0.0)
    spread_lanes = jnp.where(iota((nz // 4, nz), 1) // 4 == iota((nz // 4, nz), 0), 1.0, 0.0)
    wide = mm(mm(spread_rows, change[...]), spread_lanes)
    for x in range(bx):
        X = x // 4
        out[0, x] = ends[0, x] + wide[X * by:(X + 1) * by, :]


def project(ends, basis, coeffs, acc):
    nt, bx = ends.shape[0], ends.shape[1]
    modes = basis.shape[0]
    for n in range(nt):
        for base in range(0, modes, 16):
            def body(x, carry):
                u = ends[n, x]
                new = []
                for j in range(16):
                    p = basis[base + j, x].astype(F32) * u
                    p = (p[0:8, 0:128] + p[0:8, 128:256]) + (p[8:16, 0:128] + p[8:16, 128:256])
                    new.append(carry[j] + p)
                return tuple(new)
            sums = lax.fori_loop(0, bx, body, tuple(jnp.zeros((8, 128), F32) for _ in range(16)))
            for j in range(16):
                acc[n * modes + base + j:n * modes + base + j + 1, :] = jnp.sum(sums[j], axis=0, keepdims=True)
    ones = jnp.ones((8, 128), F32)
    coeffs[...] = lax.dot_general(ones, acc[...], (((1,), (1,)), ((), ())), precision=HIGH, preferred_element_type=F32)


def coarse_step(c, k0):
    k = k0 * (1.0 + 0.5 * jnp.tanh(c))
    total = jnp.zeros_like(c)
    for dim in range(3):
        n = c.shape[dim]
        ka, kb = lax.slice_in_dim(k, 0, n - 1, axis=dim), lax.slice_in_dim(k, 1, n, axis=dim)
        f = conduct_exact(ka, kb) * (lax.slice_in_dim(c, 1, n, axis=dim) - lax.slice_in_dim(c, 0, n - 1, axis=dim))
        after = [(0, 0)] * 3
        before = [(0, 0)] * 3
        after[dim], before[dim] = (0, 1), (1, 0)
        total += jnp.pad(f, after) - jnp.pad(f, before)
    return c + (2.0 * coarse_rate) * total


def local(sizes, slice_starts, material, conduct_table, wall_flags, pod_basis):
    nt, ngx, ngy = sizes
    bx, by, nz = material.shape
    modes = pod_basis.shape[0]
    cx, cy, cz = bx // 4, by // 4, nz // 4
    crows = cx * cy
    extended = pltpu.VMEM((bx + 2 * W, by + 2 * YP, nz), F32)
    dma = pltpu.SemaphoreType.DMA
    vmem = pl.BlockSpec(memory_space=pltpu.VMEM)
    fine_end, means = pl.pallas_call(
        functools.partial(kernel, sizes),
        out_shape=(jax.ShapeDtypeStruct(slice_starts.shape, F32), jax.ShapeDtypeStruct((3 * crows, 128), F32)),
        in_specs=[vmem, vmem, pl.BlockSpec(memory_space=pltpu.SMEM), vmem],
        out_specs=(vmem, vmem),
        scratch_shapes=[extended] * 7 + [dma((3, 8)), dma((3, 8))],
        compiler_params=pltpu.CompilerParams(collective_id=0, has_side_effects=True, vmem_limit_bytes=32 * 1024 * 1024),
    )(slice_starts, material, conduct_table, wall_flags)
    every = lax.all_gather(means, ("tm", "gx", "gy"), axis=0, tiled=False)
    every = every.reshape(nt, ngx, ngy, 3, cx, cy, 128)[..., :cz]
    every = every.transpose(3, 0, 1, 4, 2, 5, 6).reshape(3, nt, ngx * cx, ngy * cy, cz)
    coef = every[1, 0]
    starts = every[0]
    moved = jax.vmap(lambda c: coarse_step(c, coef))(starts)
    current = starts[0]
    changes = []
    for n in range(nt):
        ahead = coarse_step(current, coef)
        changes.append(ahead - moved[n])
        current = changes[n] + every[2, n]
    t, gx, gy = lax.axis_index("tm"), lax.axis_index("gx"), lax.axis_index("gy")
    change = lax.dynamic_slice(jnp.stack(changes), (t, gx * cx, gy * cy, 0), (1, cx, cy, cz)).reshape(crows, cz)
    ends = pl.pallas_call(
        functools.partial(finish, cy),
        out_shape=jax.ShapeDtypeStruct(slice_starts.shape, F32),
        in_specs=[vmem, vmem],
        out_specs=vmem,
    )(fine_end, change)
    gathered = lax.all_gather(ends, "tm", axis=0, tiled=True)
    sums = pl.pallas_call(
        project,
        out_shape=jax.ShapeDtypeStruct((8, nt * modes), F32),
        in_specs=[vmem, vmem],
        out_specs=vmem,
        scratch_shapes=[pltpu.VMEM((nt * modes, 128), F32)],
        compiler_params=pltpu.CompilerParams(vmem_limit_bytes=32 * 1024 * 1024),
    )(gathered, pod_basis)
    return ends, lax.psum(sums[0].reshape(nt, modes), ("gx", "gy"))


def solution(mesh):
    in_specs = (
        P("tm", "gx", "gy", None),
        P("gx", "gy", None),
        P(),
        P(None, "gx", "gy"),
        P("tm", "gx", "gy", None),
    )
    out_specs = (P("tm", "gx", "gy", None), P(None, "tm"))
    sizes = tuple(mesh.shape[name] for name in ("tm", "gx", "gy"))
    return jax.shard_map(functools.partial(local, sizes), mesh=mesh, in_specs=in_specs, out_specs=out_specs, check_vma=False)
```

```python
import functools

import jax
import jax.numpy as jnp
from jax import lax
from jax.experimental import pallas as pl
from jax.experimental.pallas import tpu as pltpu
from jax.sharding import PartitionSpec as P

STEPS = 8
W = 4
YP = 8

fine_rate = 0.1
coarse_rate = 0.05

MESH = pl.DeviceIdType.MESH
F32 = jnp.float32
HIGH = lax.Precision.HIGHEST
AROUND = [(a, b) for a in (-1, 0, 1) for b in (-1, 0, 1) if (a, b) != (0, 0)]


def conduct(k_here, k_there):
    bottom = jnp.maximum(k_here + k_there, 1.0)
    return k_here * k_there * pl.reciprocal(bottom, approx=True)


def conduct_exact(k_here, k_there):
    return k_here * k_there / jnp.maximum(k_here + k_there, 1.0)


def iota(shape, dim):
    return lax.broadcasted_iota(jnp.int32, shape, dim)


def mm(a, b):
    return lax.dot_general(a, b, (((1,), (0,)), ((), ())), precision=HIGH, preferred_element_type=F32)


def kernel(sizes, start, material, table, walls, out, means,
           A, B, C, S, SA, KG, K, h_send, h_recv):
    nt, ngx, ngy = sizes
    bx, by, nz = material.shape
    ex, ey = bx + 2 * W, by + 2 * YP
    cx, cy = bx // 4, by // 4
    crows = cx * cy
    t, gx, gy = lax.axis_index("tm"), lax.axis_index("gx"), lax.axis_index("gy")

    def exists(a, b):
        ok = None
        for d, g, n in ((a, gx, ngx), (b, gy, ngy)):
            if d:
                this = (g + d >= 0) & (g + d < n)
                ok = this if ok is None else ok & this
        return ok

    def if_there(a, b, extra=None):
        ok = exists(a, b)
        if extra is not None:
            ok = extra if ok is None else ok & extra
        return pl.when(ok) if ok is not None else (lambda f: f())

    barrier = pltpu.get_barrier_semaphore()
    for a, b in AROUND:
        @if_there(a, b)
        def _():
            pl.semaphore_signal(barrier, inc=1, device_id={"tm": t, "gx": gx + a, "gy": gy + b}, device_id_type=MESH)

    for a, xs in ((-1, slice(0, W)), (1, slice(W + bx, ex))):
        @pl.when(jnp.logical_not(exists(a, 0)))
        def _():
            for ref in (A, C, S):
                ref[xs] = jnp.zeros((W, ey, nz), F32)
    for b, ys in ((-1, slice(0, YP)), (1, slice(YP + by, ey))):
        @pl.when(jnp.logical_not(exists(0, b)))
        def _():
            for ref in (A, C, S):
                ref[:, ys, :] = jnp.zeros((ex, YP, nz), F32)
    lane = iota((by, nz), 1)
    eye = iota((by, by), 0) == iota((by, by), 1)

    @pl.loop(0, bx)
    def _(x):
        mat = material[x]
        coef = jnp.zeros((by, nz), F32)
        for region in range(table.shape[0]):
            coef = jnp.where(mat == region, table[region], coef)
        low = jnp.sum(jnp.where(eye, walls[0, pl.ds(x, 1), :].astype(F32), 0.0), axis=1, keepdims=True)
        top = jnp.sum(jnp.where(eye, walls[1, pl.ds(x, 1), :].astype(F32), 0.0), axis=1, keepdims=True)
        flag = jnp.where(lane == 0, low, jnp.where(lane == nz - 1, top, 0.0))
        S[W + x, YP:YP + by, :] = jnp.where(flag > 0.5, -coef, coef)
        A[W + x, YP:YP + by, :] = start[0, x]

    rows_p = (cx * cy, cx * by)
    gather_rows = jnp.where(
        (iota(rows_p, 0) // cy == iota(rows_p, 1) // by) & (iota(rows_p, 0) % cy == (iota(rows_p, 1) % by) // 4), 1.0, 0.0)
    gather_lanes = jnp.where(iota((nz, 128), 0) // 4 == iota((nz, 128), 1), 1.0 / 64.0, 0.0)
    def restrict(cell):
        slabs = []
        for X in range(cx):
            slabs.append((cell(4 * X) + cell(4 * X + 1)) + (cell(4 * X + 2) + cell(4 * X + 3)))
        return mm(mm(gather_rows, jnp.concatenate(slabs, axis=0)), gather_lanes)

    pl.semaphore_wait(barrier, (1 + (gx > 0).astype(jnp.int32) + (gx < ngx - 1).astype(jnp.int32))
                      * (1 + (gy > 0).astype(jnp.int32) + (gy < ngy - 1).astype(jnp.int32)) - 1)

    def halo(ref, kind, i, a, b):
        xs = {-1: (W, W + bx, W), 0: (W, W, bx), 1: (bx, 0, W)}[a]
        ys = {-1: (YP, YP + by, YP), 0: (YP, YP, by), 1: (by, 0, YP)}[b]
        return pltpu.make_async_remote_copy(
            src_ref=ref.at[pl.ds(xs[0], xs[2]), pl.ds(ys[0], ys[2]), :],
            dst_ref=ref.at[pl.ds(xs[1], xs[2]), pl.ds(ys[1], ys[2]), :],
            send_sem=h_send.at[kind, i],
            recv_sem=h_recv.at[kind, i],
            device_id={"tm": t, "gx": gx + a, "gy": gy + b},
            device_id_type=MESH,
        )

    def send_halo(ref, kind):
        for i, (a, b) in enumerate(AROUND):
            @if_there(a, b)
            def _():
                halo(ref, kind, i, a, b).start()

    def left_halo(ref, kind):
        for i, (a, b) in enumerate(AROUND):
            @if_there(a, b)
            def _():
                halo(ref, kind, i, a, b).wait_send()

    def land_halo(ref, kind):
        for i, (a, b) in enumerate(AROUND):
            @if_there(-a, -b)
            def _():
                xs = {-1: (W + bx, W), 0: (W, bx), 1: (0, W)}[a]
                ys = {-1: (YP + by, YP), 0: (YP, by), 1: (0, YP)}[b]
                spot = ref.at[pl.ds(xs[0], xs[1]), pl.ds(ys[0], ys[1]), :]
                pltpu.make_async_remote_copy(
                    src_ref=spot, dst_ref=spot, send_sem=h_send.at[kind, i], recv_sem=h_recv.at[kind, i],
                    device_id={"tm": t, "gx": gx - a, "gy": gy - b}, device_id_type=MESH,
                ).wait_recv()

    send_halo(A, 0)
    send_halo(S, 1)

    own = slice(YP, YP + by)
    means[0:crows, :] = restrict(lambda x: A[W + x, own, :])
    means[crows:2 * crows, :] = restrict(lambda x: jnp.abs(S[W + x, own, :]))

    def conductivity(src, r):
        @pl.loop(W - r - 1, W + bx + r + 1)
        def _(x):
            K[x] = SA[x] * (1.0 + 0.5 * jnp.tanh(src[x]))

    def step(src, put, r):
        conductivity(src, r)
        ylo, yhi = (YP, YP + by) if r == 0 else (YP - 4, YP + by + 4)
        rows = slice(ylo, yhi)
        last = iota((yhi - ylo, nz), 1) == nz - 1

        def body(x, carry):
            kc, uc, fxm = carry
            kn, un = K[x + 1, rows, :], src[x + 1, rows, :]
            fx = conduct(kc, kn) * (un - uc)
            total = fx - fxm
            total += conduct(kc, K[x, ylo + 1:yhi + 1, :]) * (src[x, ylo + 1:yhi + 1, :] - uc)
            total += conduct(kc, K[x, ylo - 1:yhi - 1, :]) * (src[x, ylo - 1:yhi - 1, :] - uc)
            fz = conduct(kc, pltpu.roll(kc, nz - 1, 1)) * (pltpu.roll(uc, nz - 1, 1) - uc)
            fz = jnp.where(last, 0.0, fz)
            total += fz - pltpu.roll(fz, 1, 1)
            total -= conduct(kc, KG[x, rows, :]) * uc
            put(x, rows, uc + (2.0 * fine_rate) * total)
            return kn, un, fx

        x0 = W - r
        k0, u0 = K[x0, rows, :], src[x0, rows, :]
        k1, u1 = K[x0 - 1, rows, :], src[x0 - 1, rows, :]
        lax.fori_loop(x0, W + bx + r, body, (k0, u0, conduct(k0, k1) * (u0 - u1)))

    def into(ref):
        def put(x, rows, value):
            ref[x, rows, :] = value
        return put

    def into_out(x, rows, value):
        out[0, x - W] = value

    land_halo(A, 0)
    land_halo(S, 1)

    @pl.loop(0, ex)
    def _(x):
        s = S[x]
        SA[x] = jnp.abs(s)
        KG[x] = jnp.where(s < 0.0, -s, 0.0)

    def exchange_then(src, kind):
        send_halo(src, kind)
        land_halo(src, kind)

    step(A, into(B), 3)
    left_halo(A, 0)
    step(B, into(A), 2)
    step(A, into(B), 1)
    step(B, into(C), 0)
    exchange_then(C, 2)
    step(C, into(B), 3)
    step(B, into(A), 2)
    step(A, into(B), 1)

    step(B, into_out, 0)
    means[2 * crows:, :] = restrict(lambda x: out[0, x])
    left_halo(S, 1)
    left_halo(C, 2)


def finish(cy, ends, change, out):
    bx, by, nz = ends.shape[1:]
    cx = bx // 4
    shape = (cx * by, cx * cy)
    spread_rows = jnp.where(
        (iota(shape, 1) // cy == iota(shape, 0) // by) & (iota(shape, 1) % cy == (iota(shape, 0) % by) // 4), 1.0, 0.0)
    spread_lanes = jnp.where(iota((nz // 4, nz), 1) // 4 == iota((nz // 4, nz), 0), 1.0, 0.0)
    wide = mm(mm(spread_rows, change[...]), spread_lanes)
    for x in range(bx):
        X = x // 4
        out[0, x] = ends[0, x] + wide[X * by:(X + 1) * by, :]


def project(ends, basis, coeffs, acc):
    nt, bx = ends.shape[0], ends.shape[1]
    modes = basis.shape[0]
    for n in range(nt):
        for base in range(0, modes, 16):
            def body(x, carry):
                u = ends[n, x]
                new = []
                for j in range(16):
                    p = basis[base + j, x].astype(F32) * u
                    p = (p[0:8, 0:128] + p[0:8, 128:256]) + (p[8:16, 0:128] + p[8:16, 128:256])
                    new.append(carry[j] + p)
                return tuple(new)
            sums = lax.fori_loop(0, bx, body, tuple(jnp.zeros((8, 128), F32) for _ in range(16)))
            for j in range(16):
                acc[n * modes + base + j:n * modes + base + j + 1, :] = jnp.sum(sums[j], axis=0, keepdims=True)
    ones = jnp.ones((8, 128), F32)
    coeffs[...] = lax.dot_general(ones, acc[...], (((1,), (1,)), ((), ())), precision=HIGH, preferred_element_type=F32)


def coarse_step(c, k0):
    k = k0 * (1.0 + 0.5 * jnp.tanh(c))
    total = jnp.zeros_like(c)
    for dim in range(3):
        n = c.shape[dim]
        ka, kb = lax.slice_in_dim(k, 0, n - 1, axis=dim), lax.slice_in_dim(k, 1, n, axis=dim)
        f = conduct_exact(ka, kb) * (lax.slice_in_dim(c, 1, n, axis=dim) - lax.slice_in_dim(c, 0, n - 1, axis=dim))
        after = [(0, 0)] * 3
        before = [(0, 0)] * 3
        after[dim], before[dim] = (0, 1), (1, 0)
        total += jnp.pad(f, after) - jnp.pad(f, before)
    return c + (2.0 * coarse_rate) * total


def local(sizes, slice_starts, material, conduct_table, wall_flags, pod_basis):
    nt, ngx, ngy = sizes
    bx, by, nz = material.shape
    modes = pod_basis.shape[0]
    cx, cy, cz = bx // 4, by // 4, nz // 4
    crows = cx * cy
    extended = pltpu.VMEM((bx + 2 * W, by + 2 * YP, nz), F32)
    dma = pltpu.SemaphoreType.DMA
    vmem = pl.BlockSpec(memory_space=pltpu.VMEM)
    fine_end, means = pl.pallas_call(
        functools.partial(kernel, sizes),
        out_shape=(jax.ShapeDtypeStruct(slice_starts.shape, F32), jax.ShapeDtypeStruct((3 * crows, 128), F32)),
        in_specs=[vmem, vmem, pl.BlockSpec(memory_space=pltpu.SMEM), vmem],
        out_specs=(vmem, vmem),
        scratch_shapes=[extended] * 7 + [dma((3, 8)), dma((3, 8))],
        compiler_params=pltpu.CompilerParams(collective_id=0, has_side_effects=True, vmem_limit_bytes=32 * 1024 * 1024),
    )(slice_starts, material, conduct_table, wall_flags)
    every = lax.all_gather(means, "tm", axis=0, tiled=True)
    every = lax.all_gather(every, ("gx", "gy"), axis=0, tiled=True)
    every = every.reshape(ngx, ngy, nt, 3, cx, cy, 128)[..., :cz]
    every = every.transpose(3, 2, 0, 4, 1, 5, 6).reshape(3, nt, ngx * cx, ngy * cy, cz)
    coef = every[1, 0]
    starts = every[0]
    moved = jax.vmap(lambda c: coarse_step(c, coef))(starts)
    current = starts[0]
    changes = []
    for n in range(nt):
        ahead = coarse_step(current, coef)
        changes.append(ahead - moved[n])
        current = changes[n] + every[2, n]
    t, gx, gy = lax.axis_index("tm"), lax.axis_index("gx"), lax.axis_index("gy")
    change = lax.dynamic_slice(jnp.stack(changes), (t, gx * cx, gy * cy, 0), (1, cx, cy, cz)).reshape(crows, cz)
    ends = pl.pallas_call(
        functools.partial(finish, cy),
        out_shape=jax.ShapeDtypeStruct(slice_starts.shape, F32),
        in_specs=[vmem, vmem],
        out_specs=vmem,
    )(fine_end, change)
    gathered = lax.all_gather(ends, "tm", axis=0, tiled=True)
    sums = pl.pallas_call(
        project,
        out_shape=jax.ShapeDtypeStruct((8, nt * modes), F32),
        in_specs=[vmem, vmem],
        out_specs=vmem,
        scratch_shapes=[pltpu.VMEM((nt * modes, 128), F32)],
        compiler_params=pltpu.CompilerParams(vmem_limit_bytes=32 * 1024 * 1024),
    )(gathered, pod_basis)
    return ends, lax.psum(sums[0].reshape(nt, modes), ("gx", "gy"))


def solution(mesh):
    in_specs = (
        P("tm", "gx", "gy", None),
        P("gx", "gy", None),
        P(),
        P(None, "gx", "gy"),
        P("tm", "gx", "gy", None),
    )
    out_specs = (P("tm", "gx", "gy", None), P(None, "tm"))
    sizes = tuple(mesh.shape[name] for name in ("tm", "gx", "gy"))
    return jax.shard_map(functools.partial(local, sizes), mesh=mesh, in_specs=in_specs, out_specs=out_specs, check_vma=False)
```
